32 devices in a mesh: groups: 2 (over y), seq: 16 (over z, x, core).
Axes of the slice: x: 2, y: 2, z: 4, core: 2. Of those that a mesh axis runs over, the one named last changes fastest.
Arguments:
- features: bfloat16 [2, 16384, 1408], P('groups', 'seq'), parts along dimension 0, may hold values from -600 to 600
- norm_gain: float32 [1408], replicated, may hold values from 0.1 to 1.9
- conv_weight: bfloat16 [5, 1408, 1536], P(None, None, 'seq'), may hold values from -0.0625 to 0.0625
- pair_projection: bfloat16 [1536, 512], replicated, may hold values from -0.15625 to 0.15625
- outer_weight: bfloat16 [128, 128], replicated, may hold values from -0.5 to 0.5
- row_gate: bfloat16 [128, 128], replicated, may hold values from -0.5 to 0.5
- row_output: bfloat16 [128, 128], replicated, may hold values from -0.5 to 0.5
- column_gate: bfloat16 [128, 128], replicated, may hold values from -0.5 to 0.5
- column_output: bfloat16 [128, 128], replicated, may hold values from -0.5 to 0.5
Outputs:
- trunk: bfloat16 [2, 8192, 1536], P('groups', 'seq'), parts along dimension 0
- pair: bfloat16 [2, 512, 512, 128], P('groups', 'seq'), parts along dimension 0
The draws below stay inside these ranges and needn't reach their ends.
There are 2 independent parts, one for each index of `groups`. The reference program is written for one: setup_inputs(seed, part) draws one part's arguments, and reference() takes and returns one part's arrays. A program takes and returns all parts, laid end to end along the dimension named above; an argument that names none is the same for every part. Nothing has to cross between parts.
All inputs are finite; a program needn't handle non-finite values.
Results may differ from the reference program's by a relative error of at most 0.0095.
Values may be sent and summed in bfloat16 or wider, within the bound.
A program may use at most 192 MiB of HBM per device.

```python
import math
import jax
import jax.numpy as jnp
from jax import lax

CIN = 1408
COUT = 1536
CP = 128
KW = 5
TOK = 512
W = 1
LEN = 16384
HALF = 8192
SPAN = 256


def draw_features(key, part):
    first, second, third = jax.random.split(key, 3)
    base = jnp.clip(jax.random.normal(first, (W, LEN, CIN), jnp.float32), -6.0, 6.0)
    row_scale = jnp.exp(jax.random.uniform(second, (W, LEN, 1), jnp.float32, 0.0, math.log(10.0)))
    channel_scale = jnp.exp(jax.random.uniform(third, (1, 1, CIN), jnp.float32, 0.0, math.log(10.0)))
    return (base * row_scale * channel_scale).astype(jnp.bfloat16)


def levels(stream_key, shape, shards, smallest, largest):
    def one(dim, blocks):
        heights = jax.random.uniform(jax.random.fold_in(jax.random.fold_in(stream_key, 6), dim), (blocks,), jnp.float32, smallest / len(shards), largest / len(shards))
        return jnp.repeat(jnp.exp(heights), shape[dim] // blocks).reshape((-1,) + (1,) * (len(shape) - dim - 1))

    gain = one(*shards[0])
    for cut in shards[1:]:
        gain = gain * one(*cut)
    return gain


def centred(key, shape, deviation, most, pieces=(), kind=jnp.bfloat16):
    loudness = levels(key, shape, pieces, -0.22, 0.18) if pieces else 1.0
    drawn = jax.random.normal(key, shape, jnp.float32) * deviation * loudness
    return jnp.minimum(jnp.maximum(drawn, -most), most).astype(kind)


def setup_inputs(seed: int = 0, part: int = 0) -> dict:
    keys = jax.random.split(jax.random.key(seed), 10)
    part_keys = jax.random.split(jax.random.fold_in(keys[9], part), 10)
    return {
        "features": draw_features(jax.random.fold_in(jax.random.fold_in(keys[9], part), 71), part),
        "norm_gain": jnp.clip(1.0 + 0.18 * jax.random.normal(keys[1], (CIN,), jnp.float32), 0.1, 1.9),
        "conv_weight": centred(keys[2], (KW, CIN, COUT), (KW * CIN) ** -0.5, 0.0625, ((2, 16),)),
        "pair_projection": centred(keys[3], (COUT, 4 * CP), COUT ** -0.5, 0.15625),
        "outer_weight": centred(keys[4], (CP, CP), CP ** -0.5, 0.5),
        "row_gate": centred(keys[5], (CP, CP), CP ** -0.5, 0.5),
        "row_output": centred(keys[6], (CP, CP), CP ** -0.5, 0.5),
        "column_gate": centred(keys[7], (CP, CP), CP ** -0.5, 0.5),
        "column_output": centred(keys[8], (CP, CP), CP ** -0.5, 0.5),
    }


def layer_norm(values):
    center = values - lax.optimization_barrier(jnp.mean(values, axis=-1, keepdims=True))
    return center * lax.rsqrt(lax.optimization_barrier(jnp.mean(center * center, axis=-1, keepdims=True)) + 1e-05)

def distance_kernel(row_index, column_index, reach):
    return jnp.exp(-jnp.abs(row_index[:, None] - column_index[None, :]) / reach).astype(jnp.bfloat16)

def reference(features, norm_gain, conv_weight, pair_projection, outer_weight, row_gate, row_output, column_gate, column_output):
    positions = jnp.arange(TOK, dtype=jnp.float32)
    kernel = distance_kernel(positions, positions, jnp.float32(SPAN)).astype(jnp.float32)
    row_total = lax.optimization_barrier(jnp.sum(kernel, axis=1))
    column_total = lax.optimization_barrier(jnp.sum(kernel, axis=0))
    filters = conv_weight.astype(jnp.float32)
    gains = norm_gain.astype(jnp.float32)
    highest = lax.Precision.HIGHEST

    def window(sample):
        values = sample.astype(jnp.float32)
        scaled = values * lax.rsqrt(lax.optimization_barrier(jnp.mean(values * values, axis=-1, keepdims=True)) + 1e-06) * gains
        activated = jax.nn.gelu(scaled).astype(jnp.bfloat16)
        padded = jnp.pad(activated.astype(jnp.float32), ((KW // 2, KW // 2), (0, 0)))
        convolved = jnp.zeros((LEN, COUT), jnp.float32)
        for offset in range(KW):
            convolved = convolved + jnp.dot(padded[offset:offset + LEN], filters[offset], precision=highest)
        trunk = lax.optimization_barrier(jnp.max(convolved.reshape(HALF, 2, COUT), axis=1)).astype(jnp.bfloat16)
        tokens = lax.optimization_barrier(jnp.mean(trunk.astype(jnp.float32).reshape(TOK, HALF // TOK, COUT), axis=1)).astype(jnp.bfloat16)
        projected = jnp.dot(tokens, pair_projection, preferred_element_type=jnp.float32)
        left = projected[:, :CP]
        right = projected[:, CP:2 * CP].astype(jnp.bfloat16)
        start_term = projected[:, 2 * CP:3 * CP]
        end_term = projected[:, 3 * CP:].astype(jnp.bfloat16)
        outer = (left[:, None, :] * right.astype(jnp.float32)[None, :, :]).astype(jnp.bfloat16)
        initial = jnp.einsum('ijc,cd->ijd', outer.astype(jnp.float32), outer_weight.astype(jnp.float32), precision=highest)
        initial = initial + start_term[:, None, :] + end_term.astype(jnp.float32)[None, :, :]
        normed = layer_norm(initial).astype(jnp.bfloat16).astype(jnp.float32)
        row_mean = (jnp.einsum('ij,ijc->ic', kernel, normed, precision=highest) / row_total[:, None]).astype(jnp.bfloat16)
        row_term = jnp.dot(row_mean, row_output, preferred_element_type=jnp.float32)
        row_weight = jax.nn.sigmoid(jnp.einsum('ijc,cd->ijd', normed, row_gate.astype(jnp.float32), precision=highest))
        after_rows = (initial + row_weight * row_term[:, None, :]).astype(jnp.bfloat16)
        column_normed = layer_norm(after_rows.astype(jnp.float32)).astype(jnp.bfloat16).astype(jnp.float32)
        column_mean = (jnp.einsum('ij,ijc->jc', kernel, column_normed, precision=highest) / column_total[:, None]).astype(jnp.bfloat16)
        column_term = jnp.dot(column_mean, column_output, preferred_element_type=jnp.float32)
        column_weight = jax.nn.sigmoid(jnp.einsum('ijc,cd->ijd', column_normed, column_gate.astype(jnp.float32), precision=highest))
        pair = (after_rows.astype(jnp.float32) + column_weight * column_term[None, :, :]).astype(jnp.bfloat16)
        return (trunk, pair)
    trunk, pair = lax.map(window, features)
    return (trunk, pair)
```

```python
import functools

import jax
import jax.numpy as jnp
from jax import lax
from jax.experimental import pallas as pl
from jax.experimental.pallas import tpu as pltpu
from jax.sharding import PartitionSpec as P

KW = 5
MESH = pl.DeviceIdType.MESH


def padded_2(x, sides, width):
    for axis, dim in sides:
        peers, length = (lax.axis_size(axis), x.shape[dim])
        up = [(i, (i + 1) % peers) for i in range(peers - 1)]
        down = [(j, i) for i, j in up]
        last = lax.slice_in_dim(x, length - width, length, axis=dim)
        leading = lax.slice_in_dim(x, 0, width, axis=dim)
        before = lax.ppermute(last, axis, up)
        after = lax.ppermute(leading, axis, down)
        x = jnp.concatenate([before, x, after], axis=dim)
    return x


def layer_norm(values):
    center = values - jnp.mean(values, axis=-1, keepdims=True)
    return center * lax.rsqrt(jnp.mean(center * center, axis=-1, keepdims=True) + 1e-05)


def distance_kernel(row_index, column_index, reach):
    return jnp.exp(-jnp.abs(row_index[:, None] - column_index[None, :]) / reach).astype(
        jnp.bfloat16
    )


SPAN = 256.0


def pair_kernel(peers, tokens, proj_ref, ow_ref, rg_ref, ro_ref, cg_ref, co_ref, out_ref,
                terms, init, normed, after, rmean, rterm, psum, sums, cmean, cterm, lefts, starts,
                send_a, recv_a, send_b, recv_b, send_c, recv_c):
    group = lax.axis_index("groups")
    me = lax.axis_index("seq")
    rows = tokens // peers
    bf16, f32 = jnp.bfloat16, jnp.float32
    barrier = pltpu.get_barrier_semaphore()
    for k in range(1, peers):
        pl.semaphore_signal(barrier, inc=1, device_id=(group, lax.rem(me + k, peers)),
                            device_id_type=MESH)
    terms[me] = jnp.concatenate([proj_ref[:, 128:256], proj_ref[:, 384:512]], axis=1).astype(bf16)
    lefts[...] = proj_ref[:, 0:128]
    starts[...] = proj_ref[:, 256:384]
    pl.semaphore_wait(barrier, peers - 1)

    def exchange(source, target, send, recv):
        copies = []
        for k in range(1, peers):
            peer = lax.rem(me + k, peers)
            copies.append(pltpu.make_async_remote_copy(
                src_ref=source(peer), dst_ref=target, send_sem=send.at[k], recv_sem=recv.at[k],
                device_id=(group, peer), device_id_type=MESH))
            copies[-1].start()
        return copies

    def finish(copies):
        for copy in copies:
            copy.wait()

    def norm(v):
        center = v - jnp.mean(v, axis=-1, keepdims=True)
        return (center * lax.rsqrt(jnp.mean(center * center, axis=-1, keepdims=True) + 1e-05)).astype(bf16)

    half = tokens // 2

    def weights(i, b):
        j = lax.broadcasted_iota(jnp.int32, (half, 128), 0) + (b * half)
        gap = jnp.abs(j - (me * rows + i)).astype(f32)
        return jnp.exp(-gap / SPAN).astype(bf16).astype(f32)

    finish(exchange(lambda peer: terms.at[me], terms.at[me], send_a, recv_a))

    def first(i, carry):
        total = jnp.zeros((1, 128), f32)
        wsum = jnp.zeros((1, 128), f32)
        for b in range(2):
            part = terms[pl.ds(b * (peers // 2), peers // 2)].reshape(half, 256).astype(f32)
            left = lefts[pl.ds(i, 1)]
            start = starts[pl.ds(i, 1)]
            outer = (left * part[:, :128]).astype(bf16)
            value = jnp.dot(outer, ow_ref[...], preferred_element_type=f32)
            value = value + start + part[:, 128:]
            init[i, pl.ds(b * half, half)] = value
            n = norm(value)
            normed[i, pl.ds(b * half, half)] = n
            w = weights(i, b)
            total = total + jnp.sum(w * n.astype(f32), axis=0, keepdims=True)
            wsum = wsum + jnp.sum(w, axis=0, keepdims=True)
        rmean[pl.ds(i, 1)] = total / wsum
        return carry

    lax.fori_loop(0, rows, first, 0)
    rterm[...] = jnp.dot(rmean[...].astype(bf16), ro_ref[...], preferred_element_type=f32)
    psum[...] = jnp.zeros_like(psum)

    def second(i, carry):
        for b in range(2):
            at = pl.ds(b * half, half)
            gate = 0.5 * jnp.tanh(0.5 * jnp.dot(normed[i, at], rg_ref[...], preferred_element_type=f32)) + 0.5
            value = (init[i, at] + gate * rterm[pl.ds(i, 1)]).astype(bf16)
            after[i, at] = value
            n = norm(value.astype(f32))
            normed[i, at] = n
            psum[at] = psum[at] + weights(i, b) * n.astype(f32)
        return carry

    lax.fori_loop(0, rows, second, 0)

    def block(peer):
        return pl.ds(pl.multiple_of(peer * rows, rows), rows)

    copies = exchange(lambda peer: psum.at[block(peer)], sums.at[me], send_b, recv_b)

    def third(i, carry):
        for b in range(2):
            at = pl.ds(b * half, half)
            init[i, at] = 0.5 * jnp.tanh(0.5 * jnp.dot(normed[i, at], cg_ref[...], preferred_element_type=f32)) + 0.5
        return carry

    lax.fori_loop(0, rows // 2, third, 0)
    sums[me] = psum[block(me)]
    finish(copies)
    total = jnp.sum(sums[...], axis=0)
    row_at = lax.broadcasted_iota(jnp.int32, (rows, tokens), 0) + me * rows
    gap = jnp.abs(row_at - lax.broadcasted_iota(jnp.int32, (rows, tokens), 1)).astype(f32)
    wsum = jnp.sum(jnp.exp(-gap / SPAN).astype(bf16).astype(f32), axis=1, keepdims=True)
    cmean[me] = (total / wsum).astype(bf16)
    copies = exchange(lambda peer: cmean.at[me], cmean.at[me], send_c, recv_c)
    lax.fori_loop(rows // 2, rows, third, 0)
    finish(copies)
    cterm[...] = jnp.dot(cmean[...].reshape(tokens, 128), co_ref[...], preferred_element_type=f32)

    def fourth(i, carry):
        out_ref[i] = (after[i].astype(f32) + init[i] * cterm[...]).astype(bf16)
        return carry

    lax.fori_loop(0, rows, fourth, 0)


def pair_stage(projected, ow, rg, ro, cg, co):
    peers = lax.axis_size("seq")
    rows = projected.shape[0]
    tokens = rows * peers
    f32, bf16 = jnp.float32, jnp.bfloat16
    sem = pltpu.SemaphoreType.DMA((peers,))
    return pl.pallas_call(
        functools.partial(pair_kernel, peers, tokens),
        out_shape=jax.ShapeDtypeStruct((rows, tokens, 128), bf16),
        in_specs=[pl.BlockSpec(memory_space=pltpu.VMEM)] * 6,
        out_specs=pl.BlockSpec(memory_space=pltpu.VMEM),
        scratch_shapes=[
            pltpu.VMEM((peers, rows, 256), bf16),
            pltpu.VMEM((rows, tokens, 128), f32),
            pltpu.VMEM((rows, tokens, 128), bf16),
            pltpu.VMEM((rows, tokens, 128), bf16),
            pltpu.VMEM((rows, 128), f32),
            pltpu.VMEM((rows, 128), f32),
            pltpu.VMEM((tokens, 128), f32),
            pltpu.VMEM((peers, rows, 128), f32),
            pltpu.VMEM((peers, rows, 128), bf16),
            pltpu.VMEM((tokens, 128), f32),
            pltpu.VMEM((rows, 128), f32),
            pltpu.VMEM((rows, 128), f32),
        ] + [sem] * 6,
        compiler_params=pltpu.CompilerParams(collective_id=1, has_side_effects=True,
                                             vmem_limit_bytes=48 * 1024 * 1024),
    )(projected, ow, rg, ro, cg, co)


def body(
    features,
    norm_gain,
    conv_weight,
    pair_projection,
    outer_weight,
    row_gate,
    row_output,
    column_gate,
    column_output,
):
    windows, local_bins, channels = features.shape
    values = features.astype(jnp.float32)
    scaled = (
        values * lax.rsqrt(jnp.mean(values * values, axis=-1, keepdims=True) + 1e-06) * norm_gain
    )
    activated = jax.nn.gelu(scaled).astype(jnp.bfloat16)
    padded = padded_2(activated, (("seq", 1),), KW // 2)
    piece = lax.all_gather(conv_weight, "seq", axis=2, tiled=True)
    result = jnp.einsum(
        "wrc,cn->wrn", padded[:, 0:local_bins], piece[0], preferred_element_type=jnp.float32
    )
    for offset in range(1, KW):
        result = result + jnp.einsum(
            "wrc,cn->wrn",
            padded[:, offset : offset + local_bins],
            piece[offset],
            preferred_element_type=jnp.float32,
        )
    width = piece.shape[2]
    trunk = jnp.max(result.reshape(windows, local_bins // 2, 2, width), axis=2).astype(jnp.bfloat16)
    out_channels = trunk.shape[2]
    local_rows = local_bins // 32
    tokens = jnp.mean(
        trunk.astype(jnp.float32).reshape(windows, local_rows, 16, out_channels), axis=2
    ).astype(jnp.bfloat16)
    pair_width = outer_weight.shape[0]

    def project(rows, block):
        return jnp.einsum(
            "wtc,cp->wtp",
            rows,
            pair_projection[:, block * pair_width : (block + 1) * pair_width],
            preferred_element_type=jnp.float32,
        )

    if windows == 1 and local_rows % 16 == 0 and pair_width == 128:
        projected = jnp.einsum("tc,cp->tp", tokens[0], pair_projection, preferred_element_type=jnp.float32)
        pair = pair_stage(projected, outer_weight, row_gate, row_output, column_gate, column_output)
        return (trunk, pair[None])

    left = project(tokens, 0)
    start_term = project(tokens, 2)
    all_tokens = lax.all_gather(tokens, "seq", axis=1, tiled=True)
    right = project(all_tokens, 1).astype(jnp.bfloat16)
    end_term = project(all_tokens, 3).astype(jnp.bfloat16)
    all_count = right.shape[1]
    outer = (left[:, :, None, :] * right.astype(jnp.float32)[:, None, :, :]).astype(jnp.bfloat16)
    initial = jnp.einsum("wijc,cd->wijd", outer, outer_weight, preferred_element_type=jnp.float32)
    initial = initial + start_term[:, :, None, :] + end_term.astype(jnp.float32)[:, None, :, :]
    reach = jnp.float32(SPAN)
    first_row = lax.axis_index("seq") * local_rows
    own_index = (first_row + jnp.arange(local_rows, dtype=jnp.int32)).astype(jnp.float32)
    all_index = jnp.arange(all_count, dtype=jnp.float32)
    row_kernel = distance_kernel(own_index, all_index, reach)
    row_total = jnp.sum(row_kernel.astype(jnp.float32), axis=1)
    normed = layer_norm(initial).astype(jnp.bfloat16)
    row_mean = (
        jnp.einsum("ij,wijc->wic", row_kernel, normed, preferred_element_type=jnp.float32)
        / row_total[None, :, None]
    ).astype(jnp.bfloat16)
    row_term = jnp.einsum("wic,cd->wid", row_mean, row_output, preferred_element_type=jnp.float32)
    row_weight = jax.nn.sigmoid(
        jnp.einsum("wijc,cd->wijd", normed, row_gate, preferred_element_type=jnp.float32)
    )
    after_rows = (initial + row_weight * row_term[:, :, None, :]).astype(jnp.bfloat16)
    full_kernel = distance_kernel(all_index, all_index, reach)
    column_total = jnp.sum(full_kernel.astype(jnp.float32), axis=0)
    column_normed = layer_norm(after_rows.astype(jnp.float32)).astype(jnp.bfloat16)
    partial_sums = jnp.einsum(
        "ij,wijc->wjc", row_kernel, column_normed, preferred_element_type=jnp.float32
    )
    column_sums = lax.psum(partial_sums, "seq")
    column_mean = (column_sums / column_total[None, :, None]).astype(jnp.bfloat16)
    column_term = jnp.einsum(
        "wjc,cd->wjd", column_mean, column_output, preferred_element_type=jnp.float32
    )
    column_weight = jax.nn.sigmoid(
        jnp.einsum("wijc,cd->wijd", column_normed, column_gate, preferred_element_type=jnp.float32)
    )
    pair = (after_rows.astype(jnp.float32) + column_weight * column_term[:, None, :, :]).astype(
        jnp.bfloat16
    )
    return (trunk, pair)


def solution(mesh):
    in_specs = (P("groups", "seq", None), P(), P(None, None, "seq"), P(), P(), P(), P(), P(), P())
    out_specs = (P("groups", "seq", None), P("groups", "seq", None, None))
    return jax.shard_map(body, mesh=mesh, in_specs=in_specs, out_specs=out_specs, check_vma=False)
```

```python
import functools

import jax
import jax.numpy as jnp
from jax import lax
from jax.experimental import pallas as pl
from jax.experimental.pallas import tpu as pltpu
from jax.sharding import PartitionSpec as P

KW = 5
MESH = pl.DeviceIdType.MESH


def padded_2(x, sides, width):
    for axis, dim in sides:
        peers, length = (lax.axis_size(axis), x.shape[dim])
        up = [(i, (i + 1) % peers) for i in range(peers - 1)]
        down = [(j, i) for i, j in up]
        last = lax.slice_in_dim(x, length - width, length, axis=dim)
        leading = lax.slice_in_dim(x, 0, width, axis=dim)
        before = lax.ppermute(last, axis, up)
        after = lax.ppermute(leading, axis, down)
        x = jnp.concatenate([before, x, after], axis=dim)
    return x


def layer_norm(values):
    center = values - jnp.mean(values, axis=-1, keepdims=True)
    return center * lax.rsqrt(jnp.mean(center * center, axis=-1, keepdims=True) + 1e-05)


def distance_kernel(row_index, column_index, reach):
    return jnp.exp(-jnp.abs(row_index[:, None] - column_index[None, :]) / reach).astype(
        jnp.bfloat16
    )


SPAN = 256.0


def pair_kernel(peers, tokens, proj_ref, ow_ref, rg_ref, ro_ref, cg_ref, co_ref, out_ref,
                terms, init, normed, after, rmean, rterm, psum, sums, cmean, cterm, lefts, starts,
                send_a, recv_a, send_b, recv_b, send_c, recv_c):
    group = lax.axis_index("groups")
    me = lax.axis_index("seq")
    rows = tokens // peers
    bf16, f32 = jnp.bfloat16, jnp.float32
    barrier = pltpu.get_barrier_semaphore()
    for k in range(1, peers):
        pl.semaphore_signal(barrier, inc=1, device_id=(group, lax.rem(me + k, peers)),
                            device_id_type=MESH)
    terms[me] = jnp.concatenate([proj_ref[:, 128:256], proj_ref[:, 384:512]], axis=1).astype(bf16)
    lefts[...] = proj_ref[:, 0:128]
    starts[...] = proj_ref[:, 256:384]
    pl.semaphore_wait(barrier, peers - 1)

    def exchange(source, target, send, recv):
        copies = []
        for k in range(1, peers):
            peer = lax.rem(me + k, peers)
            copies.append(pltpu.make_async_remote_copy(
                src_ref=source(peer), dst_ref=target, send_sem=send.at[k], recv_sem=recv.at[k],
                device_id=(group, peer), device_id_type=MESH))
            copies[-1].start()
        return copies

    def finish(copies):
        for copy in copies:
            copy.wait()

    def norm(v):
        center = v - jnp.mean(v, axis=-1, keepdims=True)
        return (center * lax.rsqrt(jnp.mean(center * center, axis=-1, keepdims=True) + 1e-05)).astype(bf16)

    half = tokens // 2

    def weights(i, b):
        j = lax.broadcasted_iota(jnp.int32, (half, 128), 0) + (b * half)
        gap = jnp.abs(j - (me * rows + i)).astype(f32)
        return jnp.exp(-gap / SPAN).astype(bf16).astype(f32)

    finish(exchange(lambda peer: terms.at[me], terms.at[me], send_a, recv_a))

    def first(i, carry):
        total = jnp.zeros((1, 128), f32)
        wsum = jnp.zeros((1, 128), f32)
        for b in range(2):
            part = terms[pl.ds(b * (peers // 2), peers // 2)].reshape(half, 256).astype(f32)
            left = lefts[pl.ds(i, 1)]
            start = starts[pl.ds(i, 1)]
            outer = (left * part[:, :128]).astype(bf16)
            value = jnp.dot(outer, ow_ref[...], preferred_element_type=f32)
            value = value + start + part[:, 128:]
            init[i, pl.ds(b * half, half)] = value
            n = norm(value)
            normed[i, pl.ds(b * half, half)] = n
            w = weights(i, b)
            total = total + jnp.sum(w * n.astype(f32), axis=0, keepdims=True)
            wsum = wsum + jnp.sum(w, axis=0, keepdims=True)
        rmean[pl.ds(i, 1)] = total / wsum
        return carry

    lax.fori_loop(0, rows, first, 0)
    rterm[...] = jnp.dot(rmean[...].astype(bf16), ro_ref[...], preferred_element_type=f32)
    psum[...] = jnp.zeros_like(psum)

    def second(i, carry):
        for b in range(2):
            at = pl.ds(b * half, half)
            gate = 0.5 * jnp.tanh(0.5 * jnp.dot(normed[i, at], rg_ref[...], preferred_element_type=f32)) + 0.5
            value = (init[i, at] + gate * rterm[pl.ds(i, 1)]).astype(bf16)
            after[i, at] = value
            n = norm(value.astype(f32))
            normed[i, at] = n
            psum[at] = psum[at] + weights(i, b) * n.astype(f32)
        return carry

    lax.fori_loop(0, rows, second, 0)

    def block(peer):
        return pl.ds(pl.multiple_of(peer * rows, rows), rows)

    copies = exchange(lambda peer: psum.at[block(peer)], sums.at[me], send_b, recv_b)

    def third(i, carry):
        for b in range(2):
            at = pl.ds(b * half, half)
            init[i, at] = 0.5 * jnp.tanh(0.5 * jnp.dot(normed[i, at], cg_ref[...], preferred_element_type=f32)) + 0.5
        return carry

    lax.fori_loop(0, rows // 2, third, 0)
    sums[me] = psum[block(me)]
    finish(copies)
    total = jnp.sum(sums[...], axis=0)
    row_at = lax.broadcasted_iota(jnp.int32, (rows, tokens), 0) + me * rows
    gap = jnp.abs(row_at - lax.broadcasted_iota(jnp.int32, (rows, tokens), 1)).astype(f32)
    wsum = jnp.sum(jnp.exp(-gap / SPAN).astype(bf16).astype(f32), axis=1, keepdims=True)
    cmean[me] = (total / wsum).astype(bf16)
    copies = exchange(lambda peer: cmean.at[me], cmean.at[me], send_c, recv_c)
    lax.fori_loop(rows // 2, rows, third, 0)
    finish(copies)
    cterm[...] = jnp.dot(cmean[...].reshape(tokens, 128), co_ref[...], preferred_element_type=f32)

    def fourth(i, carry):
        out_ref[i] = (after[i].astype(f32) + init[i] * cterm[...]).astype(bf16)
        return carry

    lax.fori_loop(0, rows, fourth, 0)


def pair_stage(projected, ow, rg, ro, cg, co):
    peers = lax.axis_size("seq")
    rows = projected.shape[0]
    tokens = rows * peers
    f32, bf16 = jnp.float32, jnp.bfloat16
    sem = pltpu.SemaphoreType.DMA((peers,))
    return pl.pallas_call(
        functools.partial(pair_kernel, peers, tokens),
        out_shape=jax.ShapeDtypeStruct((rows, tokens, 128), bf16),
        in_specs=[pl.BlockSpec(memory_space=pltpu.VMEM)] * 6,
        out_specs=pl.BlockSpec(memory_space=pltpu.VMEM),
        scratch_shapes=[
            pltpu.VMEM((peers, rows, 256), bf16),
            pltpu.VMEM((rows, tokens, 128), f32),
            pltpu.VMEM((rows, tokens, 128), bf16),
            pltpu.VMEM((rows, tokens, 128), bf16),
            pltpu.VMEM((rows, 128), f32),
            pltpu.VMEM((rows, 128), f32),
            pltpu.VMEM((tokens, 128), f32),
            pltpu.VMEM((peers, rows, 128), f32),
            pltpu.VMEM((peers, rows, 128), bf16),
            pltpu.VMEM((tokens, 128), f32),
            pltpu.VMEM((rows, 128), f32),
            pltpu.VMEM((rows, 128), f32),
        ] + [sem] * 6,
        compiler_params=pltpu.CompilerParams(collective_id=1, has_side_effects=True,
                                             vmem_limit_bytes=48 * 1024 * 1024),
    )(projected, ow, rg, ro, cg, co)

def conv_kernel(zs, feat_ref, gain_ref, w_ref, pp_ref, trunk_ref, proj_ref,
                wall, act, shifted, acc, edge_out, edge_in, own_sem,
                zu_send, zd_send, z_recv, x_send, x_recv, y_send, y_recv, c_send, c_recv,
                e_send, e_recv):
    bf16, f32 = jnp.bfloat16, jnp.float32
    y = lax.axis_index("groups")
    me = lax.axis_index("seq")
    z, x, c = lax.div(me, 4), lax.rem(lax.div(me, 2), 2), lax.rem(me, 2)
    peers = 4 * zs
    taps, _, _, width, channels = wall.shape
    bins = feat_ref.shape[0]
    blocks = channels // 128
    third = width // 3
    wide = pl.ds(pl.multiple_of(third * y, third), 2 * third)
    mine = pl.ds(pl.multiple_of(2 * third * y, third), third)
    theirs = pl.ds(pl.multiple_of(2 * third * (1 - y), third), third)
    up, down = jnp.minimum(me + 4, peers - 1), jnp.maximum(me - 4, 0)
    side, core = me + 2 - 4 * x, me + 1 - 2 * c
    following, previous = jnp.minimum(me + 1, peers - 1), jnp.maximum(me - 1, 0)
    has_up, has_down = z < zs - 1, z > 0
    has_next, has_prev = me < peers - 1, me > 0

    barrier = pltpu.get_barrier_semaphore()

    def greet(group, peer):
        pl.semaphore_signal(barrier, inc=1, device_id=(group, peer), device_id_type=MESH)

    greet(y, side)
    greet(y, core)
    greet(1 - y, me)
    for cond, peer in ((has_up, up), (has_down, down), (has_next, following), (has_prev, previous)):
        pl.when(cond)(functools.partial(greet, y, peer))

    def own_copy(t):
        return pltpu.make_async_copy(w_ref.at[t], wall.at[t, 2 * z + x, c], own_sem.at[t])

    for t in range(taps):
        own_copy(t).start()
    count = 3 + sum(jnp.where(cond, 1, 0) for cond in (has_up, has_down, has_next, has_prev))
    pl.semaphore_wait(barrier, count)

    def remote(ref, send, recv, group, peer):
        return pltpu.make_async_remote_copy(src_ref=ref, dst_ref=ref, send_sem=send, recv_sem=recv,
                                            device_id=(group, peer), device_id_type=MESH)

    def z_copy(t, zz, upward):
        send = zu_send if upward else zd_send
        return remote(wall.at[t, 2 * zz + x, c, wide], send.at[t, zz], z_recv.at[t, zz], y,
                      up if upward else down)

    def x_copy(t, zz):
        return remote(wall.at[t, 2 * zz + x, c, wide], x_send.at[t, zz], x_recv.at[t, zz], y, side)

    def x_arrival(t, zz):
        return remote(wall.at[t, 2 * zz + 1 - x, c, wide], x_send.at[t, zz], x_recv.at[t, zz], y, side)

    def y_copy(t, unit):
        return remote(wall.at[t, unit, c, mine], y_send.at[t, unit], y_recv.at[t, unit], 1 - y, me)

    def y_arrival(t, unit):
        return remote(wall.at[t, unit, c, theirs], y_send.at[t, unit], y_recv.at[t, unit], 1 - y, me)

    def c_copy(t, h, which):
        return remote(wall.at[t, pl.ds(h * zs, zs), which], c_send.at[t, h], c_recv.at[t, h], y, core)

    def own(t):
        own_copy(t).wait()

        @pl.when(has_up)
        def _():
            z_copy(t, z, True).start()

        @pl.when(has_down)
        def _():
            z_copy(t, z, False).start()

        x_copy(t, z).start()

    def relay_z(t, d):
        @pl.when(z >= d)
        def _():
            zz = jnp.maximum(z - d, 0)
            z_copy(t, zz, True).wait_recv()

            @pl.when(has_up)
            def _():
                z_copy(t, zz, True).start()

            x_copy(t, zz).start()
            y_copy(t, 2 * zz + x).start()

        @pl.when(z + d < zs)
        def _():
            zz = jnp.minimum(z + d, zs - 1)
            z_copy(t, zz, False).wait_recv()

            @pl.when(has_down)
            def _():
                z_copy(t, zz, False).start()

            x_copy(t, zz).start()
            y_copy(t, 2 * zz + x).start()

    def relay_x(t, k):
        zz = lax.rem(z + k, zs)
        x_arrival(t, zz).wait_recv()
        y_copy(t, 2 * zz + 1 - x).start()

    def gather_y(t):
        for k in range(zs):
            zz = lax.rem(z + k, zs)
            if k:
                y_arrival(t, 2 * zz + x).wait_recv()
            y_arrival(t, 2 * zz + 1 - x).wait_recv()
        for h in range(2):
            c_copy(t, h, c).start()

    def gather_c(t, h):
        c_copy(t, h, 1 - c).wait_recv()

    def compute(t, h, m):
        n = zs * 2 * width
        filters = wall[t, zs * h:zs * h + zs].reshape(n, channels)
        at = pl.ds(h * n, n)
        acc[m, :, at] = acc[m, :, at] + lax.dot_general(
            shifted[t + m], filters, (((1,), (1,)), ((), ())), preferred_element_type=f32)

    own(0)
    own(1)

    def activate(r, carry):
        at = pl.multiple_of(r * 32, 32)
        v = feat_ref[pl.ds(at, 32)].astype(f32)
        v = v * lax.rsqrt(jnp.mean(v * v, axis=-1, keepdims=True) + 1e-06) * gain_ref[...]
        v = jax.nn.gelu(v).astype(bf16).astype(f32)
        for b in range(blocks):
            act[b, pl.ds(at + 8, 32)] = v[:, b * 128:(b + 1) * 128]
        return carry

    lax.fori_loop(0, bins // 32, activate, 0)
    for b in range(blocks):
        lanes = pl.ds(b * 128, 128)
        edge_out[0, :, lanes] = act[b, pl.ds(8 + bins - 16, 16)].astype(bf16)
        edge_out[1, :, lanes] = act[b, pl.ds(8, 16)].astype(bf16)

    def edge_copy(k):
        return pltpu.make_async_remote_copy(
            src_ref=edge_out.at[k], dst_ref=edge_in.at[k], send_sem=e_send.at[k], recv_sem=e_recv.at[k],
            device_id=(y, previous if k else following), device_id_type=MESH)

    edges = ((has_next, has_prev), (has_prev, has_next))
    for k in range(2):
        pl.when(edges[k][0])(lambda k=k: edge_copy(k).start())
        pl.when(jnp.logical_not(edges[k][1]))(lambda k=k: edge_in.__setitem__(k, jnp.zeros(edge_in.shape[1:], bf16)))
    acc[...] = jnp.zeros_like(acc)
    for d in range(1, zs):
        relay_z(0, d)
    for k in range(2):
        pl.when(edges[k][1])(lambda k=k: edge_copy(k).wait_recv())
    for b in range(blocks):
        lanes = pl.ds(b * 128, 128)
        act[b, 0:8] = edge_in[0, :, lanes].astype(f32)[8:16]
        act[b, 8 + bins:16 + bins] = edge_in[1, :, lanes].astype(f32)[0:8]

    def build(k, carry):
        for b in range(blocks):
            shifted[k, :, pl.ds(b * 128, 128)] = act[b, pl.ds(6 + k, bins // 2, stride=2)].astype(bf16)
        return carry

    for k in range(taps + 1):
        build(k, 0)
        if k < zs:
            relay_x(0, k)
    gather_y(0)

    def tap(t, carry):
        @pl.when(t < taps - 1)
        def _():
            own(t + 1)

        relay_z(t, 1)
        relay_z(t, 2)
        gather_c(t - 1, 0)
        compute(t - 1, 0, 0)
        for d in range(3, zs):
            relay_z(t, d)
        relay_x(t, 0)
        compute(t - 1, 0, 1)
        for k in range(1, zs):
            relay_x(t, k)
        gather_c(t - 1, 1)
        compute(t - 1, 1, 0)
        gather_y(t)
        compute(t - 1, 1, 1)
        return carry

    lax.fori_loop(1, taps, tap, 0)
    columns = zs * 2 * width
    total = jnp.zeros((bins // 32, pp_ref.shape[1]), f32)
    for h in range(2):
        gather_c(taps - 1, h)
        compute(taps - 1, h, 0)
        compute(taps - 1, h, 1)
        at = pl.ds(h * columns, columns)
        trunk = jnp.maximum(acc[0, :, at], acc[1, :, at]).astype(bf16)
        trunk_ref[:, at] = trunk
        tokens = jnp.mean(trunk.astype(f32).reshape(bins // 32, 16, columns), axis=1).astype(bf16)
        total = total + jnp.dot(tokens, pp_ref[at], preferred_element_type=f32)
    proj_ref[...] = total

    def drain(t, carry):
        @pl.when(has_up)
        def _():
            z_copy(t, z, True).wait_send()

        @pl.when(has_down)
        def _():
            z_copy(t, z, False).wait_send()

        x_copy(t, z).wait_send()
        y_copy(t, 2 * z + 1 - x).wait_send()
        for d in range(1, zs):
            for cond, more, upward in ((z >= d, has_up, True), (z + d < zs, has_down, False)):
                zz = jnp.clip(z - d if upward else z + d, 0, zs - 1)

                @pl.when(jnp.logical_and(cond, more))
                def _(zz=zz, upward=upward):
                    z_copy(t, zz, upward).wait_send()

            zz = lax.rem(z + d, zs)
            x_copy(t, zz).wait_send()
            y_copy(t, 2 * zz + x).wait_send()
            y_copy(t, 2 * zz + 1 - x).wait_send()
        for h in range(2):
            c_copy(t, h, c).wait_send()
        return carry

    lax.fori_loop(0, taps, drain, 0)
    for k in range(2):
        pl.when(edges[k][0])(lambda k=k: edge_copy(k).wait_send())


def conv_stage(features, gain, weight, projection):
    f32, bf16 = jnp.float32, jnp.bfloat16
    bins, channels = features.shape
    taps, width, _ = weight.shape
    peers = lax.axis_size("seq")
    zs = peers // 4
    out = width * peers
    dma = pltpu.SemaphoreType.DMA
    return pl.pallas_call(
        functools.partial(conv_kernel, zs),
        out_shape=(jax.ShapeDtypeStruct((bins // 2, out), bf16),
                   jax.ShapeDtypeStruct((bins // 32, projection.shape[1]), f32)),
        in_specs=[pl.BlockSpec(memory_space=pltpu.VMEM), pl.BlockSpec(memory_space=pltpu.VMEM),
                  pl.BlockSpec(memory_space=pl.ANY), pl.BlockSpec(memory_space=pltpu.VMEM)],
        out_specs=(pl.BlockSpec(memory_space=pltpu.VMEM), pl.BlockSpec(memory_space=pltpu.VMEM)),
        scratch_shapes=[
            pltpu.VMEM((taps, 2 * zs, 2, width, channels), bf16),
            pltpu.VMEM((channels // 128, bins + 16, 128), f32),
            pltpu.VMEM((taps + 1, bins // 2, channels), bf16),
            pltpu.VMEM((2, bins // 2, out), f32),
            pltpu.VMEM((2, 16, channels), bf16),
            pltpu.VMEM((2, 16, channels), bf16),
            dma((taps,)),
            dma((taps, zs)), dma((taps, zs)), dma((taps, zs)),
            dma((taps, zs)), dma((taps, zs)),
            dma((taps, 2 * zs)), dma((taps, 2 * zs)),
            dma((taps, 2)), dma((taps, 2)),
            dma((2,)), dma((2,)),
        ],
        compiler_params=pltpu.CompilerParams(collective_id=2, has_side_effects=True,
                                             vmem_limit_bytes=60 * 1024 * 1024),
    )(features, gain.reshape(1, channels), weight, projection)


def body(
    features,
    norm_gain,
    conv_weight,
    pair_projection,
    outer_weight,
    row_gate,
    row_output,
    column_gate,
    column_output,
):
    windows, local_bins, channels = features.shape
    width = conv_weight.shape[2]
    if (windows == 1 and local_bins % 512 == 0 and width % 96 == 0 and channels % 128 == 0
            and outer_weight.shape[0] == 128 and lax.axis_size("groups") == 2 and lax.axis_size("seq") == 16):
        trunk, projected = conv_stage(features[0], norm_gain, jnp.swapaxes(conv_weight, 1, 2), pair_projection)
        pair = pair_stage(projected, outer_weight, row_gate, row_output, column_gate, column_output)
        return (trunk[None], pair[None])
    values = features.astype(jnp.float32)
    scaled = (
        values * lax.rsqrt(jnp.mean(values * values, axis=-1, keepdims=True) + 1e-06) * norm_gain
    )
    activated = jax.nn.gelu(scaled).astype(jnp.bfloat16)
    padded = padded_2(activated, (("seq", 1),), KW // 2)
    piece = lax.all_gather(conv_weight, "seq", axis=2, tiled=True)
    result = jnp.einsum(
        "wrc,cn->wrn", padded[:, 0:local_bins], piece[0], preferred_element_type=jnp.float32
    )
    for offset in range(1, KW):
        result = result + jnp.einsum(
            "wrc,cn->wrn",
            padded[:, offset : offset + local_bins],
            piece[offset],
            preferred_element_type=jnp.float32,
        )
    width = piece.shape[2]
    trunk = jnp.max(result.reshape(windows, local_bins // 2, 2, width), axis=2).astype(jnp.bfloat16)
    out_channels = trunk.shape[2]
    local_rows = local_bins // 32
    tokens = jnp.mean(
        trunk.astype(jnp.float32).reshape(windows, local_rows, 16, out_channels), axis=2
    ).astype(jnp.bfloat16)
    pair_width = outer_weight.shape[0]

    def project(rows, block):
        return jnp.einsum(
            "wtc,cp->wtp",
            rows,
            pair_projection[:, block * pair_width : (block + 1) * pair_width],
            preferred_element_type=jnp.float32,
        )

    if windows == 1 and local_rows % 16 == 0 and pair_width == 128:
        projected = jnp.einsum("tc,cp->tp", tokens[0], pair_projection, preferred_element_type=jnp.float32)
        pair = pair_stage(projected, outer_weight, row_gate, row_output, column_gate, column_output)
        return (trunk, pair[None])

    left = project(tokens, 0)
    start_term = project(tokens, 2)
    all_tokens = lax.all_gather(tokens, "seq", axis=1, tiled=True)
    right = project(all_tokens, 1).astype(jnp.bfloat16)
    end_term = project(all_tokens, 3).astype(jnp.bfloat16)
    all_count = right.shape[1]
    outer = (left[:, :, None, :] * right.astype(jnp.float32)[:, None, :, :]).astype(jnp.bfloat16)
    initial = jnp.einsum("wijc,cd->wijd", outer, outer_weight, preferred_element_type=jnp.float32)
    initial = initial + start_term[:, :, None, :] + end_term.astype(jnp.float32)[:, None, :, :]
    reach = jnp.float32(SPAN)
    first_row = lax.axis_index("seq") * local_rows
    own_index = (first_row + jnp.arange(local_rows, dtype=jnp.int32)).astype(jnp.float32)
    all_index = jnp.arange(all_count, dtype=jnp.float32)
    row_kernel = distance_kernel(own_index, all_index, reach)
    row_total = jnp.sum(row_kernel.astype(jnp.float32), axis=1)
    normed = layer_norm(initial).astype(jnp.bfloat16)
    row_mean = (
        jnp.einsum("ij,wijc->wic", row_kernel, normed, preferred_element_type=jnp.float32)
        / row_total[None, :, None]
    ).astype(jnp.bfloat16)
    row_term = jnp.einsum("wic,cd->wid", row_mean, row_output, preferred_element_type=jnp.float32)
    row_weight = jax.nn.sigmoid(
        jnp.einsum("wijc,cd->wijd", normed, row_gate, preferred_element_type=jnp.float32)
    )
    after_rows = (initial + row_weight * row_term[:, :, None, :]).astype(jnp.bfloat16)
    full_kernel = distance_kernel(all_index, all_index, reach)
    column_total = jnp.sum(full_kernel.astype(jnp.float32), axis=0)
    column_normed = layer_norm(after_rows.astype(jnp.float32)).astype(jnp.bfloat16)
    partial_sums = jnp.einsum(
        "ij,wijc->wjc", row_kernel, column_normed, preferred_element_type=jnp.float32
    )
    column_sums = lax.psum(partial_sums, "seq")
    column_mean = (column_sums / column_total[None, :, None]).astype(jnp.bfloat16)
    column_term = jnp.einsum(
        "wjc,cd->wjd", column_mean, column_output, preferred_element_type=jnp.float32
    )
    column_weight = jax.nn.sigmoid(
        jnp.einsum("wijc,cd->wijd", column_normed, column_gate, preferred_element_type=jnp.float32)
    )
    pair = (after_rows.astype(jnp.float32) + column_weight * column_term[:, None, :, :]).astype(
        jnp.bfloat16
    )
    return (trunk, pair)


def solution(mesh):
    in_specs = (P("groups", "seq", None), P(), P(None, None, "seq"), P(), P(), P(), P(), P(), P())
    out_specs = (P("groups", "seq", None), P("groups", "seq", None, None))
    return jax.shard_map(body, mesh=mesh, in_specs=in_specs, out_specs=out_specs, check_vma=False)
```

```python
import functools

import jax
import jax.numpy as jnp
from jax import lax
from jax.experimental import pallas as pl
from jax.experimental.pallas import tpu as pltpu
from jax.sharding import PartitionSpec as P

KW = 5
MESH = pl.DeviceIdType.MESH


def padded_2(x, sides, width):
    for axis, dim in sides:
        peers, length = (lax.axis_size(axis), x.shape[dim])
        up = [(i, (i + 1) % peers) for i in range(peers - 1)]
        down = [(j, i) for i, j in up]
        last = lax.slice_in_dim(x, length - width, length, axis=dim)
        leading = lax.slice_in_dim(x, 0, width, axis=dim)
        before = lax.ppermute(last, axis, up)
        after = lax.ppermute(leading, axis, down)
        x = jnp.concatenate([before, x, after], axis=dim)
    return x


def layer_norm(values):
    center = values - jnp.mean(values, axis=-1, keepdims=True)
    return center * lax.rsqrt(jnp.mean(center * center, axis=-1, keepdims=True) + 1e-05)


def distance_kernel(row_index, column_index, reach):
    return jnp.exp(-jnp.abs(row_index[:, None] - column_index[None, :]) / reach).astype(
        jnp.bfloat16
    )


SPAN = 256.0


def pair_kernel(peers, tokens, proj_ref, ow_ref, rg_ref, ro_ref, cg_ref, co_ref, out_ref,
                terms, init, normed, after, rmean, rterm, psum, sums, cmean, cterm, lefts, starts,
                send_a, recv_a, send_b, recv_b, send_c, recv_c):
    group = lax.axis_index("groups")
    me = lax.axis_index("seq")
    rows = tokens // peers
    bf16, f32 = jnp.bfloat16, jnp.float32
    barrier = pltpu.get_barrier_semaphore()
    for k in range(1, peers):
        pl.semaphore_signal(barrier, inc=1, device_id=(group, lax.rem(me + k, peers)),
                            device_id_type=MESH)
    terms[me] = jnp.concatenate([proj_ref[:, 128:256], proj_ref[:, 384:512]], axis=1).astype(bf16)
    lefts[...] = proj_ref[:, 0:128]
    starts[...] = proj_ref[:, 256:384]
    pl.semaphore_wait(barrier, peers - 1)

    def exchange(source, target, send, recv):
        copies = []
        for k in range(1, peers):
            peer = lax.rem(me + k, peers)
            copies.append(pltpu.make_async_remote_copy(
                src_ref=source(peer), dst_ref=target, send_sem=send.at[k], recv_sem=recv.at[k],
                device_id=(group, peer), device_id_type=MESH))
            copies[-1].start()
        return copies

    def finish(copies):
        for copy in copies:
            copy.wait()

    def norm(v):
        center = v - jnp.mean(v, axis=-1, keepdims=True)
        return (center * lax.rsqrt(jnp.mean(center * center, axis=-1, keepdims=True) + 1e-05)).astype(bf16)

    half = tokens // 2

    def weights(i, b):
        j = lax.broadcasted_iota(jnp.int32, (half, 128), 0) + (b * half)
        gap = jnp.abs(j - (me * rows + i)).astype(f32)
        return jnp.exp(-gap / SPAN).astype(bf16).astype(f32)

    finish(exchange(lambda peer: terms.at[me], terms.at[me], send_a, recv_a))

    def first(i, carry):
        total = jnp.zeros((1, 128), f32)
        wsum = jnp.zeros((1, 128), f32)
        for b in range(2):
            part = terms[pl.ds(b * (peers // 2), peers // 2)].reshape(half, 256).astype(f32)
            left = lefts[pl.ds(i, 1)]
            start = starts[pl.ds(i, 1)]
            outer = (left * part[:, :128]).astype(bf16)
            value = jnp.dot(outer, ow_ref[...], preferred_element_type=f32)
            value = value + start + part[:, 128:]
            init[i, pl.ds(b * half, half)] = value
            n = norm(value)
            normed[i, pl.ds(b * half, half)] = n
            w = weights(i, b)
            total = total + jnp.sum(w * n.astype(f32), axis=0, keepdims=True)
            wsum = wsum + jnp.sum(w, axis=0, keepdims=True)
        rmean[pl.ds(i, 1)] = total / wsum
        return carry

    lax.fori_loop(0, rows, first, 0)
    rterm[...] = jnp.dot(rmean[...].astype(bf16), ro_ref[...], preferred_element_type=f32)
    psum[...] = jnp.zeros_like(psum)

    def second(i, carry):
        for b in range(2):
            at = pl.ds(b * half, half)
            gate = 0.5 * jnp.tanh(0.5 * jnp.dot(normed[i, at], rg_ref[...], preferred_element_type=f32)) + 0.5
            value = (init[i, at] + gate * rterm[pl.ds(i, 1)]).astype(bf16)
            after[i, at] = value
            n = norm(value.astype(f32))
            normed[i, at] = n
            psum[at] = psum[at] + weights(i, b) * n.astype(f32)
        return carry

    lax.fori_loop(0, rows, second, 0)

    def block(peer):
        return pl.ds(pl.multiple_of(peer * rows, rows), rows)

    copies = exchange(lambda peer: psum.at[block(peer)], sums.at[me], send_b, recv_b)

    def third(i, carry):
        for b in range(2):
            at = pl.ds(b * half, half)
            init[i, at] = 0.5 * jnp.tanh(0.5 * jnp.dot(normed[i, at], cg_ref[...], preferred_element_type=f32)) + 0.5
        return carry

    lax.fori_loop(0, rows // 2, third, 0)
    sums[me] = psum[block(me)]
    finish(copies)
    total = jnp.sum(sums[...], axis=0)
    row_at = lax.broadcasted_iota(jnp.int32, (rows, tokens), 0) + me * rows
    gap = jnp.abs(row_at - lax.broadcasted_iota(jnp.int32, (rows, tokens), 1)).astype(f32)
    wsum = jnp.sum(jnp.exp(-gap / SPAN).astype(bf16).astype(f32), axis=1, keepdims=True)
    cmean[me] = (total / wsum).astype(bf16)
    copies = exchange(lambda peer: cmean.at[me], cmean.at[me], send_c, recv_c)
    lax.fori_loop(rows // 2, rows, third, 0)
    finish(copies)
    cterm[...] = jnp.dot(cmean[...].reshape(tokens, 128), co_ref[...], preferred_element_type=f32)

    def fourth(i, carry):
        out_ref[i] = (after[i].astype(f32) + init[i] * cterm[...]).astype(bf16)
        return carry

    lax.fori_loop(0, rows, fourth, 0)


def pair_stage(projected, ow, rg, ro, cg, co):
    peers = lax.axis_size("seq")
    rows = projected.shape[0]
    tokens = rows * peers
    f32, bf16 = jnp.float32, jnp.bfloat16
    sem = pltpu.SemaphoreType.DMA((peers,))
    return pl.pallas_call(
        functools.partial(pair_kernel, peers, tokens),
        out_shape=jax.ShapeDtypeStruct((rows, tokens, 128), bf16),
        in_specs=[pl.BlockSpec(memory_space=pltpu.VMEM)] * 6,
        out_specs=pl.BlockSpec(memory_space=pltpu.VMEM),
        scratch_shapes=[
            pltpu.VMEM((peers, rows, 256), bf16),
            pltpu.VMEM((rows, tokens, 128), f32),
            pltpu.VMEM((rows, tokens, 128), bf16),
            pltpu.VMEM((rows, tokens, 128), bf16),
            pltpu.VMEM((rows, 128), f32),
            pltpu.VMEM((rows, 128), f32),
            pltpu.VMEM((tokens, 128), f32),
            pltpu.VMEM((peers, rows, 128), f32),
            pltpu.VMEM((peers, rows, 128), bf16),
            pltpu.VMEM((tokens, 128), f32),
            pltpu.VMEM((rows, 128), f32),
            pltpu.VMEM((rows, 128), f32),
        ] + [sem] * 6,
        compiler_params=pltpu.CompilerParams(collective_id=1, has_side_effects=True,
                                             vmem_limit_bytes=48 * 1024 * 1024),
    )(projected, ow, rg, ro, cg, co)

def conv_kernel(zs, feat_ref, gain_ref, w_ref, pp_ref, trunk_ref, proj_ref,
                wall, act, shifted, acc, edge_out, edge_in, own_sem,
                zu_send, zd_send, z_recv, x_send, x_recv, y_send, y_recv, c_send, c_recv,
                e_send, e_recv):
    bf16, f32 = jnp.bfloat16, jnp.float32
    y = lax.axis_index("groups")
    me = lax.axis_index("seq")
    z, x, c = lax.div(me, 4), lax.rem(lax.div(me, 2), 2), lax.rem(me, 2)
    peers = 4 * zs
    taps, _, _, width, channels = wall.shape
    bins = feat_ref.shape[0]
    blocks = channels // 128
    third = width // 3
    wide = pl.ds(pl.multiple_of(third * y, third), 2 * third)
    mine = pl.ds(pl.multiple_of(2 * third * y, third), third)
    theirs = pl.ds(pl.multiple_of(2 * third * (1 - y), third), third)
    up, down = jnp.minimum(me + 4, peers - 1), jnp.maximum(me - 4, 0)
    side, core = me + 2 - 4 * x, me + 1 - 2 * c
    following, previous = jnp.minimum(me + 1, peers - 1), jnp.maximum(me - 1, 0)
    has_up, has_down = z < zs - 1, z > 0
    has_next, has_prev = me < peers - 1, me > 0

    barrier = pltpu.get_barrier_semaphore()

    def greet(group, peer):
        pl.semaphore_signal(barrier, inc=1, device_id=(group, peer), device_id_type=MESH)

    greet(y, side)
    greet(y, core)
    greet(1 - y, me)
    for cond, peer in ((has_up, up), (has_down, down), (has_next, following), (has_prev, previous)):
        pl.when(cond)(functools.partial(greet, y, peer))

    def own_copy(t):
        return pltpu.make_async_copy(w_ref.at[t], wall.at[t, 2 * z + x, c], own_sem.at[t])

    for t in range(taps):
        own_copy(t).start()
    count = 3 + sum(jnp.where(cond, 1, 0) for cond in (has_up, has_down, has_next, has_prev))
    pl.semaphore_wait(barrier, count)

    def remote(ref, send, recv, group, peer):
        return pltpu.make_async_remote_copy(src_ref=ref, dst_ref=ref, send_sem=send, recv_sem=recv,
                                            device_id=(group, peer), device_id_type=MESH)

    def z_copy(t, zz, upward):
        send = zu_send if upward else zd_send
        return remote(wall.at[t, 2 * zz + x, c, wide], send.at[t, zz], z_recv.at[t, zz], y,
                      up if upward else down)

    def x_copy(t, zz):
        return remote(wall.at[t, 2 * zz + x, c, wide], x_send.at[t, zz], x_recv.at[t, zz], y, side)

    def x_arrival(t, zz):
        return remote(wall.at[t, 2 * zz + 1 - x, c, wide], x_send.at[t, zz], x_recv.at[t, zz], y, side)

    def y_copy(t, unit):
        return remote(wall.at[t, unit, c, mine], y_send.at[t, unit], y_recv.at[t, unit], 1 - y, me)

    def y_arrival(t, unit):
        return remote(wall.at[t, unit, c, theirs], y_send.at[t, unit], y_recv.at[t, unit], 1 - y, me)

    def c_copy(t, h, which):
        return remote(wall.at[t, pl.ds(h * zs, zs), which], c_send.at[t, h], c_recv.at[t, h], y, core)

    def own(t):
        own_copy(t).wait()

        @pl.when(has_up)
        def _():
            z_copy(t, z, True).start()

        @pl.when(has_down)
        def _():
            z_copy(t, z, False).start()

        x_copy(t, z).start()

    def relay_z(t, d):
        @pl.when(z >= d)
        def _():
            zz = jnp.maximum(z - d, 0)
            z_copy(t, zz, True).wait_recv()

            @pl.when(has_up)
            def _():
                z_copy(t, zz, True).start()

            x_copy(t, zz).start()
            y_copy(t, 2 * zz + x).start()

        @pl.when(z + d < zs)
        def _():
            zz = jnp.minimum(z + d, zs - 1)
            z_copy(t, zz, False).wait_recv()

            @pl.when(has_down)
            def _():
                z_copy(t, zz, False).start()

            x_copy(t, zz).start()
            y_copy(t, 2 * zz + x).start()

    def relay_x(t, k):
        zz = lax.rem(z + k, zs)
        x_arrival(t, zz).wait_recv()
        y_copy(t, 2 * zz + 1 - x).start()

    def gather_y(t):
        for k in range(zs):
            zz = lax.rem(z + k, zs)
            if k:
                y_arrival(t, 2 * zz + x).wait_recv()
            y_arrival(t, 2 * zz + 1 - x).wait_recv()
        for h in range(2):
            c_copy(t, h, c).start()

    def gather_c(t, h):
        c_copy(t, h, 1 - c).wait_recv()

    def compute(t, h, m):
        n = zs * 2 * width
        filters = wall[t, zs * h:zs * h + zs].reshape(n, channels)
        at = pl.ds(h * n, n)
        acc[m, :, at] = acc[m, :, at] + lax.dot_general(
            shifted[t + m], filters, (((1,), (1,)), ((), ())), preferred_element_type=f32)

    own(0)
    own(1)
    own(2)

    def activate(r, carry):
        at = pl.multiple_of(r * 32, 32)
        v = feat_ref[pl.ds(at, 32)].astype(f32)
        v = v * lax.rsqrt(jnp.mean(v * v, axis=-1, keepdims=True) + 1e-06) * gain_ref[...]
        v = jax.nn.gelu(v).astype(bf16).astype(f32)
        for b in range(blocks):
            act[b, pl.ds(at + 8, 32)] = v[:, b * 128:(b + 1) * 128]
        return carry

    lax.fori_loop(0, bins // 32, activate, 0)
    for b in range(blocks):
        lanes = pl.ds(b * 128, 128)
        edge_out[0, :, lanes] = act[b, pl.ds(8 + bins - 16, 16)].astype(bf16)
        edge_out[1, :, lanes] = act[b, pl.ds(8, 16)].astype(bf16)

    def edge_copy(k):
        return pltpu.make_async_remote_copy(
            src_ref=edge_out.at[k], dst_ref=edge_in.at[k], send_sem=e_send.at[k], recv_sem=e_recv.at[k],
            device_id=(y, previous if k else following), device_id_type=MESH)

    edges = ((has_next, has_prev), (has_prev, has_next))
    for k in range(2):
        pl.when(edges[k][0])(lambda k=k: edge_copy(k).start())
        pl.when(jnp.logical_not(edges[k][1]))(lambda k=k: edge_in.__setitem__(k, jnp.zeros(edge_in.shape[1:], bf16)))
    acc[...] = jnp.zeros_like(acc)
    for d in range(1, zs):
        relay_z(0, d)
    for k in range(2):
        pl.when(edges[k][1])(lambda k=k: edge_copy(k).wait_recv())
    for b in range(blocks):
        lanes = pl.ds(b * 128, 128)
        act[b, 0:8] = edge_in[0, :, lanes].astype(f32)[8:16]
        act[b, 8 + bins:16 + bins] = edge_in[1, :, lanes].astype(f32)[0:8]

    def build(k, carry):
        for b in range(blocks):
            shifted[k, :, pl.ds(b * 128, 128)] = act[b, pl.ds(6 + k, bins // 2, stride=2)].astype(bf16)
        return carry

    for k in range(taps + 1):
        build(k, 0)
        if k < zs - 1:
            relay_z(1, k + 1)
        if k < zs:
            relay_x(0, k)

    def stage(s, carry):
        @pl.when(s + 2 < taps)
        def _():
            own(s + 2)

        @pl.when(s + 1 < taps)
        def _():
            relay_z(s + 1, 1)

        @pl.when(s < taps)
        def _():
            for k in range(zs):
                relay_x(s, k)

        @pl.when(s >= 2)
        def _():
            gather_c(s - 2, 0)
            compute(s - 2, 0, 0)

        @pl.when(s + 1 < taps)
        def _():
            for d in range(2, zs):
                relay_z(s + 1, d)

        @pl.when(s >= 2)
        def _():
            compute(s - 2, 0, 1)

        gather_y(s - 1)

        @pl.when(s >= 2)
        def _():
            gather_c(s - 2, 1)
            compute(s - 2, 1, 0)
            compute(s - 2, 1, 1)
        return carry

    lax.fori_loop(1, taps + 1, stage, 0)
    columns = zs * 2 * width
    total = jnp.zeros((bins // 32, pp_ref.shape[1]), f32)
    for h in range(2):
        gather_c(taps - 1, h)
        compute(taps - 1, h, 0)
        compute(taps - 1, h, 1)
        at = pl.ds(h * columns, columns)
        trunk = jnp.maximum(acc[0, :, at], acc[1, :, at]).astype(bf16)
        trunk_ref[:, at] = trunk
        tokens = jnp.mean(trunk.astype(f32).reshape(bins // 32, 16, columns), axis=1).astype(bf16)
        total = total + jnp.dot(tokens, pp_ref[at], preferred_element_type=f32)
    proj_ref[...] = total

    def drain(t, carry):
        @pl.when(has_up)
        def _():
            z_copy(t, z, True).wait_send()

        @pl.when(has_down)
        def _():
            z_copy(t, z, False).wait_send()

        x_copy(t, z).wait_send()
        y_copy(t, 2 * z + 1 - x).wait_send()
        for d in range(1, zs):
            for cond, more, upward in ((z >= d, has_up, True), (z + d < zs, has_down, False)):
                zz = jnp.clip(z - d if upward else z + d, 0, zs - 1)

                @pl.when(jnp.logical_and(cond, more))
                def _(zz=zz, upward=upward):
                    z_copy(t, zz, upward).wait_send()

            zz = lax.rem(z + d, zs)
            x_copy(t, zz).wait_send()
            y_copy(t, 2 * zz + x).wait_send()
            y_copy(t, 2 * zz + 1 - x).wait_send()
        for h in range(2):
            c_copy(t, h, c).wait_send()
        return carry

    lax.fori_loop(0, taps, drain, 0)
    for k in range(2):
        pl.when(edges[k][0])(lambda k=k: edge_copy(k).wait_send())


def conv_stage(features, gain, weight, projection):
    f32, bf16 = jnp.float32, jnp.bfloat16
    bins, channels = features.shape
    taps, width, _ = weight.shape
    peers = lax.axis_size("seq")
    zs = peers // 4
    out = width * peers
    dma = pltpu.SemaphoreType.DMA
    return pl.pallas_call(
        functools.partial(conv_kernel, zs),
        out_shape=(jax.ShapeDtypeStruct((bins // 2, out), bf16),
                   jax.ShapeDtypeStruct((bins // 32, projection.shape[1]), f32)),
        in_specs=[pl.BlockSpec(memory_space=pltpu.VMEM), pl.BlockSpec(memory_space=pltpu.VMEM),
                  pl.BlockSpec(memory_space=pl.ANY), pl.BlockSpec(memory_space=pltpu.VMEM)],
        out_specs=(pl.BlockSpec(memory_space=pltpu.VMEM), pl.BlockSpec(memory_space=pltpu.VMEM)),
        scratch_shapes=[
            pltpu.VMEM((taps, 2 * zs, 2, width, channels), bf16),
            pltpu.VMEM((channels // 128, bins + 16, 128), f32),
            pltpu.VMEM((taps + 1, bins // 2, channels), bf16),
            pltpu.VMEM((2, bins // 2, out), f32),
            pltpu.VMEM((2, 16, channels), bf16),
            pltpu.VMEM((2, 16, channels), bf16),
            dma((taps,)),
            dma((taps, zs)), dma((taps, zs)), dma((taps, zs)),
            dma((taps, zs)), dma((taps, zs)),
            dma((taps, 2 * zs)), dma((taps, 2 * zs)),
            dma((taps, 2)), dma((taps, 2)),
            dma((2,)), dma((2,)),
        ],
        compiler_params=pltpu.CompilerParams(collective_id=2, has_side_effects=True,
                                             vmem_limit_bytes=60 * 1024 * 1024),
    )(features, gain.reshape(1, channels), weight, projection)


def body(
    features,
    norm_gain,
    conv_weight,
    pair_projection,
    outer_weight,
    row_gate,
    row_output,
    column_gate,
    column_output,
):
    windows, local_bins, channels = features.shape
    width = conv_weight.shape[2]
    if (windows == 1 and local_bins % 512 == 0 and width % 96 == 0 and channels % 128 == 0
            and outer_weight.shape[0] == 128 and lax.axis_size("groups") == 2 and lax.axis_size("seq") == 16):
        trunk, projected = conv_stage(features[0], norm_gain, jnp.swapaxes(conv_weight, 1, 2), pair_projection)
        pair = pair_stage(projected, outer_weight, row_gate, row_output, column_gate, column_output)
        return (trunk[None], pair[None])
    values = features.astype(jnp.float32)
    scaled = (
        values * lax.rsqrt(jnp.mean(values * values, axis=-1, keepdims=True) + 1e-06) * norm_gain
    )
    activated = jax.nn.gelu(scaled).astype(jnp.bfloat16)
    padded = padded_2(activated, (("seq", 1),), KW // 2)
    piece = lax.all_gather(conv_weight, "seq", axis=2, tiled=True)
    result = jnp.einsum(
        "wrc,cn->wrn", padded[:, 0:local_bins], piece[0], preferred_element_type=jnp.float32
    )
    for offset in range(1, KW):
        result = result + jnp.einsum(
            "wrc,cn->wrn",
            padded[:, offset : offset + local_bins],
            piece[offset],
            preferred_element_type=jnp.float32,
        )
    width = piece.shape[2]
    trunk = jnp.max(result.reshape(windows, local_bins // 2, 2, width), axis=2).astype(jnp.bfloat16)
    out_channels = trunk.shape[2]
    local_rows = local_bins // 32
    tokens = jnp.mean(
        trunk.astype(jnp.float32).reshape(windows, local_rows, 16, out_channels), axis=2
    ).astype(jnp.bfloat16)
    pair_width = outer_weight.shape[0]

    def project(rows, block):
        return jnp.einsum(
            "wtc,cp->wtp",
            rows,
            pair_projection[:, block * pair_width : (block + 1) * pair_width],
            preferred_element_type=jnp.float32,
        )

    if windows == 1 and local_rows % 16 == 0 and pair_width == 128:
        projected = jnp.einsum("tc,cp->tp", tokens[0], pair_projection, preferred_element_type=jnp.float32)
        pair = pair_stage(projected, outer_weight, row_gate, row_output, column_gate, column_output)
        return (trunk, pair[None])

    left = project(tokens, 0)
    start_term = project(tokens, 2)
    all_tokens = lax.all_gather(tokens, "seq", axis=1, tiled=True)
    right = project(all_tokens, 1).astype(jnp.bfloat16)
    end_term = project(all_tokens, 3).astype(jnp.bfloat16)
    all_count = right.shape[1]
    outer = (left[:, :, None, :] * right.astype(jnp.float32)[:, None, :, :]).astype(jnp.bfloat16)
    initial = jnp.einsum("wijc,cd->wijd", outer, outer_weight, preferred_element_type=jnp.float32)
    initial = initial + start_term[:, :, None, :] + end_term.astype(jnp.float32)[:, None, :, :]
    reach = jnp.float32(SPAN)
    first_row = lax.axis_index("seq") * local_rows
    own_index = (first_row + jnp.arange(local_rows, dtype=jnp.int32)).astype(jnp.float32)
    all_index = jnp.arange(all_count, dtype=jnp.float32)
    row_kernel = distance_kernel(own_index, all_index, reach)
    row_total = jnp.sum(row_kernel.astype(jnp.float32), axis=1)
    normed = layer_norm(initial).astype(jnp.bfloat16)
    row_mean = (
        jnp.einsum("ij,wijc->wic", row_kernel, normed, preferred_element_type=jnp.float32)
        / row_total[None, :, None]
    ).astype(jnp.bfloat16)
    row_term = jnp.einsum("wic,cd->wid", row_mean, row_output, preferred_element_type=jnp.float32)
    row_weight = jax.nn.sigmoid(
        jnp.einsum("wijc,cd->wijd", normed, row_gate, preferred_element_type=jnp.float32)
    )
    after_rows = (initial + row_weight * row_term[:, :, None, :]).astype(jnp.bfloat16)
    full_kernel = distance_kernel(all_index, all_index, reach)
    column_total = jnp.sum(full_kernel.astype(jnp.float32), axis=0)
    column_normed = layer_norm(after_rows.astype(jnp.float32)).astype(jnp.bfloat16)
    partial_sums = jnp.einsum(
        "ij,wijc->wjc", row_kernel, column_normed, preferred_element_type=jnp.float32
    )
    column_sums = lax.psum(partial_sums, "seq")
    column_mean = (column_sums / column_total[None, :, None]).astype(jnp.bfloat16)
    column_term = jnp.einsum(
        "wjc,cd->wjd", column_mean, column_output, preferred_element_type=jnp.float32
    )
    column_weight = jax.nn.sigmoid(
        jnp.einsum("wijc,cd->wijd", column_normed, column_gate, preferred_element_type=jnp.float32)
    )
    pair = (after_rows.astype(jnp.float32) + column_weight * column_term[:, None, :, :]).astype(
        jnp.bfloat16
    )
    return (trunk, pair)


def solution(mesh):
    in_specs = (P("groups", "seq", None), P(), P(None, None, "seq"), P(), P(), P(), P(), P(), P())
    out_specs = (P("groups", "seq", None), P("groups", "seq", None, None))
    return jax.shard_map(body, mesh=mesh, in_specs=in_specs, out_specs=out_specs, check_vma=False)
```

```python
import functools

import jax
import jax.numpy as jnp
from jax import lax
from jax.experimental import pallas as pl
from jax.experimental.pallas import tpu as pltpu
from jax.sharding import PartitionSpec as P

KW = 5
MESH = pl.DeviceIdType.MESH


def padded_2(x, sides, width):
    for axis, dim in sides:
        peers, length = (lax.axis_size(axis), x.shape[dim])
        up = [(i, (i + 1) % peers) for i in range(peers - 1)]
        down = [(j, i) for i, j in up]
        last = lax.slice_in_dim(x, length - width, length, axis=dim)
        leading = lax.slice_in_dim(x, 0, width, axis=dim)
        before = lax.ppermute(last, axis, up)
        after = lax.ppermute(leading, axis, down)
        x = jnp.concatenate([before, x, after], axis=dim)
    return x


def layer_norm(values):
    center = values - jnp.mean(values, axis=-1, keepdims=True)
    return center * lax.rsqrt(jnp.mean(center * center, axis=-1, keepdims=True) + 1e-05)


def distance_kernel(row_index, column_index, reach):
    return jnp.exp(-jnp.abs(row_index[:, None] - column_index[None, :]) / reach).astype(
        jnp.bfloat16
    )


SPAN = 256.0


def pair_kernel(peers, tokens, proj_ref, ow_ref, rg_ref, ro_ref, cg_ref, co_ref, out_ref,
                terms, init, normed, after, rmean, rterm, psum, sums, cmean, cterm, lefts, starts, table, rweight,
                send_a, recv_a, send_b, recv_b, send_c, recv_c):
    group = lax.axis_index("groups")
    me = lax.axis_index("seq")
    rows = tokens // peers
    bf16, f32 = jnp.bfloat16, jnp.float32
    barrier = pltpu.get_barrier_semaphore()
    for k in range(1, peers):
        pl.semaphore_signal(barrier, inc=1, device_id=(group, lax.rem(me + k, peers)),
                            device_id_type=MESH)
    terms[me] = jnp.concatenate([proj_ref[:, 128:256], proj_ref[:, 384:512]], axis=1).astype(bf16)
    lefts[...] = proj_ref[:, 0:128]
    starts[...] = proj_ref[:, 256:384]
    pl.semaphore_wait(barrier, peers - 1)

    def exchange(source, target, send, recv):
        copies = []
        for k in range(1, peers):
            peer = lax.rem(me + k, peers)
            copies.append(pltpu.make_async_remote_copy(
                src_ref=source(peer), dst_ref=target, send_sem=send.at[k], recv_sem=recv.at[k],
                device_id=(group, peer), device_id_type=MESH))
            copies[-1].start()
        return copies

    def finish(copies):
        for copy in copies:
            copy.wait()

    ones = jnp.full((256, 128), 1.0 / 128, bf16)

    def mean(v):
        high = v.astype(bf16)
        low = (v - high.astype(f32)).astype(bf16)
        return jnp.dot(jnp.concatenate([high, low], axis=1), ones, preferred_element_type=f32)

    def norm(v, average):
        center = v - average
        return (center * lax.rsqrt(mean(center * center) + 1e-05)).astype(bf16)

    half = tokens // 2

    gap = jnp.abs(lax.broadcasted_iota(jnp.int32, (2 * tokens, 128), 0) - tokens).astype(f32)
    table[...] = jnp.exp(-gap / SPAN).astype(bf16).astype(f32)
    row_at = lax.broadcasted_iota(jnp.int32, (rows, tokens), 0) + me * rows
    gap = jnp.abs(row_at - lax.broadcasted_iota(jnp.int32, (rows, tokens), 1)).astype(f32)
    near = jnp.exp(-gap / SPAN).astype(bf16)
    wsum = jnp.sum(near.astype(f32), axis=1, keepdims=True)
    rweight[...] = jnp.broadcast_to(near.astype(f32)[:, None, :], (rows, 16, tokens)).astype(bf16)

    def weights(i, b):
        return table[pl.ds(tokens - (me * rows + i) + b * half, half)]

    finish(exchange(lambda peer: terms.at[me], terms.at[me], send_a, recv_a))

    def first(i, carry):
        total = jnp.zeros((16, 128), f32)
        for b in range(2):
            part = terms[pl.ds(b * (peers // 2), peers // 2)].reshape(half, 256).astype(f32)
            left = lefts[pl.ds(i, 1)]
            start = starts[pl.ds(i, 1)]
            outer = (left * part[:, :128]).astype(bf16)
            value = jnp.dot(outer, ow_ref[...], preferred_element_type=f32)
            value = value + start + part[:, 128:]
            init[i, pl.ds(b * half, half)] = value
            n = norm(value, mean(value))
            normed[i, pl.ds(b * half, half)] = n
            total = total + jnp.dot(rweight[i, :, b * half:(b + 1) * half], n, preferred_element_type=f32)
        rmean[pl.ds(i, 1)] = total[0:1]
        return carry

    lax.fori_loop(0, rows, first, 0)
    rterm[...] = jnp.dot((rmean[...] / wsum).astype(bf16), ro_ref[...], preferred_element_type=f32)
    psum[...] = jnp.zeros_like(psum)

    def second(i, carry):
        for b in range(2):
            at = pl.ds(b * half, half)
            gate = 0.5 * jnp.tanh(0.5 * jnp.dot(normed[i, at], rg_ref[...], preferred_element_type=f32)) + 0.5
            value = (init[i, at] + gate * rterm[pl.ds(i, 1)]).astype(bf16)
            after[i, at] = value
            n = norm(value.astype(f32), jnp.dot(value, ones[:128], preferred_element_type=f32))
            normed[i, at] = n
            psum[at] = psum[at] + weights(i, b) * n.astype(f32)
        return carry

    lax.fori_loop(0, rows, second, 0)

    def block(peer):
        return pl.ds(pl.multiple_of(peer * rows, rows), rows)

    copies = exchange(lambda peer: psum.at[block(peer)], sums.at[me], send_b, recv_b)

    def third(i, carry):
        for b in range(2):
            at = pl.ds(b * half, half)
            init[i, at] = 0.5 * jnp.tanh(0.5 * jnp.dot(normed[i, at], cg_ref[...], preferred_element_type=f32)) + 0.5
        return carry

    lax.fori_loop(0, rows // 2, third, 0)
    sums[me] = psum[block(me)]
    finish(copies)
    total = jnp.sum(sums[...], axis=0)
    cmean[me] = (total / wsum).astype(bf16)
    copies = exchange(lambda peer: cmean.at[me], cmean.at[me], send_c, recv_c)
    lax.fori_loop(rows // 2, rows, third, 0)
    finish(copies)
    cterm[...] = jnp.dot(cmean[...].reshape(tokens, 128), co_ref[...], preferred_element_type=f32)

    def fourth(i, carry):
        out_ref[i] = (after[i].astype(f32) + init[i] * cterm[...]).astype(bf16)
        return carry

    lax.fori_loop(0, rows, fourth, 0)


def pair_stage(projected, ow, rg, ro, cg, co):
    peers = lax.axis_size("seq")
    rows = projected.shape[0]
    tokens = rows * peers
    f32, bf16 = jnp.float32, jnp.bfloat16
    sem = pltpu.SemaphoreType.DMA((peers,))
    return pl.pallas_call(
        functools.partial(pair_kernel, peers, tokens),
        out_shape=jax.ShapeDtypeStruct((rows, tokens, 128), bf16),
        in_specs=[pl.BlockSpec(memory_space=pltpu.VMEM)] * 6,
        out_specs=pl.BlockSpec(memory_space=pltpu.VMEM),
        scratch_shapes=[
            pltpu.VMEM((peers, rows, 256), bf16),
            pltpu.VMEM((rows, tokens, 128), f32),
            pltpu.VMEM((rows, tokens, 128), bf16),
            pltpu.VMEM((rows, tokens, 128), bf16),
            pltpu.VMEM((rows, 128), f32),
            pltpu.VMEM((rows, 128), f32),
            pltpu.VMEM((tokens, 128), f32),
            pltpu.VMEM((peers, rows, 128), f32),
            pltpu.VMEM((peers, rows, 128), bf16),
            pltpu.VMEM((tokens, 128), f32),
            pltpu.VMEM((rows, 128), f32),
            pltpu.VMEM((rows, 128), f32),
            pltpu.VMEM((2 * tokens, 128), f32),
            pltpu.VMEM((rows, 16, tokens), bf16),
        ] + [sem] * 6,
        compiler_params=pltpu.CompilerParams(collective_id=1, has_side_effects=True,
                                             vmem_limit_bytes=48 * 1024 * 1024),
    )(projected, ow, rg, ro, cg, co)

def conv_kernel(zs, feat_ref, gain_ref, w_ref, pp_ref, trunk_ref, proj_ref,
                wall, act, shifted, acc, edge_out, edge_in, own_sem,
                zu_send, zd_send, z_recv, x_send, x_recv, y_send, y_recv, c_send, c_recv,
                e_send, e_recv):
    bf16, f32 = jnp.bfloat16, jnp.float32
    y = lax.axis_index("groups")
    me = lax.axis_index("seq")
    z, x, c = lax.div(me, 4), lax.rem(lax.div(me, 2), 2), lax.rem(me, 2)
    peers = 4 * zs
    taps, _, _, width, channels = wall.shape
    bins = feat_ref.shape[0]
    blocks = channels // 128
    third = width // 3
    wide = pl.ds(pl.multiple_of(third * y, third), 2 * third)
    mine = pl.ds(pl.multiple_of(2 * third * y, third), third)
    theirs = pl.ds(pl.multiple_of(2 * third * (1 - y), third), third)
    up, down = jnp.minimum(me + 4, peers - 1), jnp.maximum(me - 4, 0)
    side, core = me + 2 - 4 * x, me + 1 - 2 * c
    following, previous = jnp.minimum(me + 1, peers - 1), jnp.maximum(me - 1, 0)
    has_up, has_down = z < zs - 1, z > 0
    has_next, has_prev = me < peers - 1, me > 0

    barrier = pltpu.get_barrier_semaphore()

    def greet(group, peer):
        pl.semaphore_signal(barrier, inc=1, device_id=(group, peer), device_id_type=MESH)

    greet(y, side)
    greet(y, core)
    greet(1 - y, me)
    for cond, peer in ((has_up, up), (has_down, down), (has_next, following), (has_prev, previous)):
        pl.when(cond)(functools.partial(greet, y, peer))

    def own_copy(t):
        return pltpu.make_async_copy(w_ref.at[t], wall.at[t, 2 * z + x, c], own_sem.at[t])

    for t in range(taps):
        own_copy(t).start()
    count = 3 + sum(jnp.where(cond, 1, 0) for cond in (has_up, has_down, has_next, has_prev))
    pl.semaphore_wait(barrier, count)

    def remote(ref, send, recv, group, peer):
        return pltpu.make_async_remote_copy(src_ref=ref, dst_ref=ref, send_sem=send, recv_sem=recv,
                                            device_id=(group, peer), device_id_type=MESH)

    def z_copy(t, zz, upward):
        send = zu_send if upward else zd_send
        return remote(wall.at[t, 2 * zz + x, c, wide], send.at[t, zz], z_recv.at[t, zz], y,
                      up if upward else down)

    def x_copy(t, zz):
        return remote(wall.at[t, 2 * zz + x, c, wide], x_send.at[t, zz], x_recv.at[t, zz], y, side)

    def x_arrival(t, zz):
        return remote(wall.at[t, 2 * zz + 1 - x, c, wide], x_send.at[t, zz], x_recv.at[t, zz], y, side)

    def y_copy(t, unit):
        return remote(wall.at[t, unit, c, mine], y_send.at[t, unit], y_recv.at[t, unit], 1 - y, me)

    def y_arrival(t, unit):
        return remote(wall.at[t, unit, c, theirs], y_send.at[t, unit], y_recv.at[t, unit], 1 - y, me)

    def c_copy(t, h, which):
        return remote(wall.at[t, pl.ds(h * zs, zs), which], c_send.at[t, h], c_recv.at[t, h], y, core)

    def own(t):
        own_copy(t).wait()

        @pl.when(has_up)
        def _():
            z_copy(t, z, True).start()

        @pl.when(has_down)
        def _():
            z_copy(t, z, False).start()

        x_copy(t, z).start()

    def relay_z(t, d):
        @pl.when(z >= d)
        def _():
            zz = jnp.maximum(z - d, 0)
            z_copy(t, zz, True).wait_recv()

            @pl.when(has_up)
            def _():
                z_copy(t, zz, True).start()

            x_copy(t, zz).start()
            y_copy(t, 2 * zz + x).start()

        @pl.when(z + d < zs)
        def _():
            zz = jnp.minimum(z + d, zs - 1)
            z_copy(t, zz, False).wait_recv()

            @pl.when(has_down)
            def _():
                z_copy(t, zz, False).start()

            x_copy(t, zz).start()
            y_copy(t, 2 * zz + x).start()

    def relay_x(t, k):
        zz = lax.rem(z + k, zs)
        x_arrival(t, zz).wait_recv()
        y_copy(t, 2 * zz + 1 - x).start()

    def gather_y(t):
        for k in range(zs):
            zz = lax.rem(z + k, zs)
            if k:
                y_arrival(t, 2 * zz + x).wait_recv()
            y_arrival(t, 2 * zz + 1 - x).wait_recv()
        for h in range(2):
            c_copy(t, h, c).start()

    def gather_c(t, h):
        c_copy(t, h, 1 - c).wait_recv()

    def compute(t, h, m):
        n = zs * 2 * width
        filters = wall[t, zs * h:zs * h + zs].reshape(n, channels)
        at = pl.ds(h * n, n)
        acc[m, :, at] = acc[m, :, at] + lax.dot_general(
            shifted[t + m], filters, (((1,), (1,)), ((), ())), preferred_element_type=f32)

    own(0)
    own(1)
    own(2)

    def activate(r, carry):
        at = pl.multiple_of(r * 32, 32)
        v = feat_ref[pl.ds(at, 32)].astype(f32)
        v = v * lax.rsqrt(jnp.mean(v * v, axis=-1, keepdims=True) + 1e-06) * gain_ref[...]
        v = jax.nn.gelu(v).astype(bf16).astype(f32)
        for b in range(blocks):
            act[b, pl.ds(at + 8, 32)] = v[:, b * 128:(b + 1) * 128]
        return carry

    lax.fori_loop(0, bins // 32, activate, 0)
    for b in range(blocks):
        lanes = pl.ds(b * 128, 128)
        edge_out[0, :, lanes] = act[b, pl.ds(8 + bins - 16, 16)].astype(bf16)
        edge_out[1, :, lanes] = act[b, pl.ds(8, 16)].astype(bf16)

    def edge_copy(k):
        return pltpu.make_async_remote_copy(
            src_ref=edge_out.at[k], dst_ref=edge_in.at[k], send_sem=e_send.at[k], recv_sem=e_recv.at[k],
            device_id=(y, previous if k else following), device_id_type=MESH)

    edges = ((has_next, has_prev), (has_prev, has_next))
    for k in range(2):
        pl.when(edges[k][0])(lambda k=k: edge_copy(k).start())
        pl.when(jnp.logical_not(edges[k][1]))(lambda k=k: edge_in.__setitem__(k, jnp.zeros(edge_in.shape[1:], bf16)))
    acc[...] = jnp.zeros_like(acc)
    for d in range(1, zs):
        relay_z(0, d)
    for k in range(2):
        pl.when(edges[k][1])(lambda k=k: edge_copy(k).wait_recv())
    for b in range(blocks):
        lanes = pl.ds(b * 128, 128)
        act[b, 0:8] = edge_in[0, :, lanes].astype(f32)[8:16]
        act[b, 8 + bins:16 + bins] = edge_in[1, :, lanes].astype(f32)[0:8]

    def build(k, carry):
        for b in range(blocks):
            shifted[k, :, pl.ds(b * 128, 128)] = act[b, pl.ds(6 + k, bins // 2, stride=2)].astype(bf16)
        return carry

    for k in range(taps + 1):
        build(k, 0)
        if k < zs - 1:
            relay_z(1, k + 1)
        if k < zs:
            relay_x(0, k)

    def stage(s, carry):
        @pl.when(s + 2 < taps)
        def _():
            own(s + 2)

        @pl.when(s + 1 < taps)
        def _():
            relay_z(s + 1, 1)

        @pl.when(s < taps)
        def _():
            for k in range(zs):
                relay_x(s, k)

        @pl.when(s >= 2)
        def _():
            gather_c(s - 2, 0)
            compute(s - 2, 0, 0)

        @pl.when(s + 1 < taps)
        def _():
            for d in range(2, zs):
                relay_z(s + 1, d)

        @pl.when(s >= 2)
        def _():
            compute(s - 2, 0, 1)

        gather_y(s - 1)

        @pl.when(s >= 2)
        def _():
            gather_c(s - 2, 1)
            compute(s - 2, 1, 0)
            compute(s - 2, 1, 1)
        return carry

    lax.fori_loop(1, taps + 1, stage, 0)
    columns = zs * 2 * width
    total = jnp.zeros((bins // 32, pp_ref.shape[1]), f32)
    for h in range(2):
        gather_c(taps - 1, h)
        compute(taps - 1, h, 0)
        compute(taps - 1, h, 1)
        at = pl.ds(h * columns, columns)
        trunk = jnp.maximum(acc[0, :, at], acc[1, :, at]).astype(bf16)
        trunk_ref[:, at] = trunk
        tokens = jnp.mean(trunk.astype(f32).reshape(bins // 32, 16, columns), axis=1).astype(bf16)
        total = total + jnp.dot(tokens, pp_ref[at], preferred_element_type=f32)
    proj_ref[...] = total

    def drain(t, carry):
        @pl.when(has_up)
        def _():
            z_copy(t, z, True).wait_send()

        @pl.when(has_down)
        def _():
            z_copy(t, z, False).wait_send()

        x_copy(t, z).wait_send()
        y_copy(t, 2 * z + 1 - x).wait_send()
        for d in range(1, zs):
            for cond, more, upward in ((z >= d, has_up, True), (z + d < zs, has_down, False)):
                zz = jnp.clip(z - d if upward else z + d, 0, zs - 1)

                @pl.when(jnp.logical_and(cond, more))
                def _(zz=zz, upward=upward):
                    z_copy(t, zz, upward).wait_send()

            zz = lax.rem(z + d, zs)
            x_copy(t, zz).wait_send()
            y_copy(t, 2 * zz + x).wait_send()
            y_copy(t, 2 * zz + 1 - x).wait_send()
        for h in range(2):
            c_copy(t, h, c).wait_send()
        return carry

    lax.fori_loop(0, taps, drain, 0)
    for k in range(2):
        pl.when(edges[k][0])(lambda k=k: edge_copy(k).wait_send())


def conv_stage(features, gain, weight, projection):
    f32, bf16 = jnp.float32, jnp.bfloat16
    bins, channels = features.shape
    taps, width, _ = weight.shape
    peers = lax.axis_size("seq")
    zs = peers // 4
    out = width * peers
    dma = pltpu.SemaphoreType.DMA
    return pl.pallas_call(
        functools.partial(conv_kernel, zs),
        out_shape=(jax.ShapeDtypeStruct((bins // 2, out), bf16),
                   jax.ShapeDtypeStruct((bins // 32, projection.shape[1]), f32)),
        in_specs=[pl.BlockSpec(memory_space=pltpu.VMEM), pl.BlockSpec(memory_space=pltpu.VMEM),
                  pl.BlockSpec(memory_space=pl.ANY), pl.BlockSpec(memory_space=pltpu.VMEM)],
        out_specs=(pl.BlockSpec(memory_space=pltpu.VMEM), pl.BlockSpec(memory_space=pltpu.VMEM)),
        scratch_shapes=[
            pltpu.VMEM((taps, 2 * zs, 2, width, channels), bf16),
            pltpu.VMEM((channels // 128, bins + 16, 128), f32),
            pltpu.VMEM((taps + 1, bins // 2, channels), bf16),
            pltpu.VMEM((2, bins // 2, out), f32),
            pltpu.VMEM((2, 16, channels), bf16),
            pltpu.VMEM((2, 16, channels), bf16),
            dma((taps,)),
            dma((taps, zs)), dma((taps, zs)), dma((taps, zs)),
            dma((taps, zs)), dma((taps, zs)),
            dma((taps, 2 * zs)), dma((taps, 2 * zs)),
            dma((taps, 2)), dma((taps, 2)),
            dma((2,)), dma((2,)),
        ],
        compiler_params=pltpu.CompilerParams(collective_id=2, has_side_effects=True,
                                             vmem_limit_bytes=60 * 1024 * 1024),
    )(features, gain.reshape(1, channels), weight, projection)


def body(
    features,
    norm_gain,
    conv_weight,
    pair_projection,
    outer_weight,
    row_gate,
    row_output,
    column_gate,
    column_output,
):
    windows, local_bins, channels = features.shape
    width = conv_weight.shape[2]
    if (windows == 1 and local_bins % 512 == 0 and width % 96 == 0 and channels % 128 == 0
            and outer_weight.shape[0] == 128 and lax.axis_size("groups") == 2 and lax.axis_size("seq") == 16):
        trunk, projected = conv_stage(features[0], norm_gain, jnp.swapaxes(conv_weight, 1, 2), pair_projection)
        pair = pair_stage(projected, outer_weight, row_gate, row_output, column_gate, column_output)
        return (trunk[None], pair[None])
    values = features.astype(jnp.float32)
    scaled = (
        values * lax.rsqrt(jnp.mean(values * values, axis=-1, keepdims=True) + 1e-06) * norm_gain
    )
    activated = jax.nn.gelu(scaled).astype(jnp.bfloat16)
    padded = padded_2(activated, (("seq", 1),), KW // 2)
    piece = lax.all_gather(conv_weight, "seq", axis=2, tiled=True)
    result = jnp.einsum(
        "wrc,cn->wrn", padded[:, 0:local_bins], piece[0], preferred_element_type=jnp.float32
    )
    for offset in range(1, KW):
        result = result + jnp.einsum(
            "wrc,cn->wrn",
            padded[:, offset : offset + local_bins],
            piece[offset],
            preferred_element_type=jnp.float32,
        )
    width = piece.shape[2]
    trunk = jnp.max(result.reshape(windows, local_bins // 2, 2, width), axis=2).astype(jnp.bfloat16)
    out_channels = trunk.shape[2]
    local_rows = local_bins // 32
    tokens = jnp.mean(
        trunk.astype(jnp.float32).reshape(windows, local_rows, 16, out_channels), axis=2
    ).astype(jnp.bfloat16)
    pair_width = outer_weight.shape[0]

    def project(rows, block):
        return jnp.einsum(
            "wtc,cp->wtp",
            rows,
            pair_projection[:, block * pair_width : (block + 1) * pair_width],
            preferred_element_type=jnp.float32,
        )

    if windows == 1 and local_rows % 16 == 0 and pair_width == 128:
        projected = jnp.einsum("tc,cp->tp", tokens[0], pair_projection, preferred_element_type=jnp.float32)
        pair = pair_stage(projected, outer_weight, row_gate, row_output, column_gate, column_output)
        return (trunk, pair[None])

    left = project(tokens, 0)
    start_term = project(tokens, 2)
    all_tokens = lax.all_gather(tokens, "seq", axis=1, tiled=True)
    right = project(all_tokens, 1).astype(jnp.bfloat16)
    end_term = project(all_tokens, 3).astype(jnp.bfloat16)
    all_count = right.shape[1]
    outer = (left[:, :, None, :] * right.astype(jnp.float32)[:, None, :, :]).astype(jnp.bfloat16)
    initial = jnp.einsum("wijc,cd->wijd", outer, outer_weight, preferred_element_type=jnp.float32)
    initial = initial + start_term[:, :, None, :] + end_term.astype(jnp.float32)[:, None, :, :]
    reach = jnp.float32(SPAN)
    first_row = lax.axis_index("seq") * local_rows
    own_index = (first_row + jnp.arange(local_rows, dtype=jnp.int32)).astype(jnp.float32)
    all_index = jnp.arange(all_count, dtype=jnp.float32)
    row_kernel = distance_kernel(own_index, all_index, reach)
    row_total = jnp.sum(row_kernel.astype(jnp.float32), axis=1)
    normed = layer_norm(initial).astype(jnp.bfloat16)
    row_mean = (
        jnp.einsum("ij,wijc->wic", row_kernel, normed, preferred_element_type=jnp.float32)
        / row_total[None, :, None]
    ).astype(jnp.bfloat16)
    row_term = jnp.einsum("wic,cd->wid", row_mean, row_output, preferred_element_type=jnp.float32)
    row_weight = jax.nn.sigmoid(
        jnp.einsum("wijc,cd->wijd", normed, row_gate, preferred_element_type=jnp.float32)
    )
    after_rows = (initial + row_weight * row_term[:, :, None, :]).astype(jnp.bfloat16)
    full_kernel = distance_kernel(all_index, all_index, reach)
    column_total = jnp.sum(full_kernel.astype(jnp.float32), axis=0)
    column_normed = layer_norm(after_rows.astype(jnp.float32)).astype(jnp.bfloat16)
    partial_sums = jnp.einsum(
        "ij,wijc->wjc", row_kernel, column_normed, preferred_element_type=jnp.float32
    )
    column_sums = lax.psum(partial_sums, "seq")
    column_mean = (column_sums / column_total[None, :, None]).astype(jnp.bfloat16)
    column_term = jnp.einsum(
        "wjc,cd->wjd", column_mean, column_output, preferred_element_type=jnp.float32
    )
    column_weight = jax.nn.sigmoid(
        jnp.einsum("wijc,cd->wijd", column_normed, column_gate, preferred_element_type=jnp.float32)
    )
    pair = (after_rows.astype(jnp.float32) + column_weight * column_term[:, None, :, :]).astype(
        jnp.bfloat16
    )
    return (trunk, pair)


def solution(mesh):
    in_specs = (P("groups", "seq", None), P(), P(None, None, "seq"), P(), P(), P(), P(), P(), P())
    out_specs = (P("groups", "seq", None), P("groups", "seq", None, None))
    return jax.shard_map(body, mesh=mesh, in_specs=in_specs, out_specs=out_specs, check_vma=False)
```
